32 devices in a mesh: panel: 8 (over z, x), prb: 4 (over y, core).
Axes of the slice: x: 2, y: 2, z: 4, core: 2. Of those that a mesh axis runs over, the one named last changes fastest.
Arguments:
- channel: bfloat16 [112, 64, 64, 128], P('panel', 'prb'), may hold values from -0.1875 to 0.1875
- received: bfloat16 [112, 64, 64, 288], P('panel', 'prb'), may hold values from -6 to 6
- keep_list: int32 [112, 64, 3], P('panel', 'prb'), may hold values from 0 to 4, as said below
- alloc: int32 [64, 64], replicated, may hold values from 0 to 511, all different within a row
- noise_var: float32 [512], replicated, may hold values from 0.1 to 1
- owner: int32 [64, 64, 1], replicated, may hold values from 0 to 31; in each aligned block of 128 rows (0 to 127, 128 to 255, ..., all dimensions but the last counted through in order) at most 8 rows name the same one
Outputs:
- equalized: float32 [8192, 288], P(('panel', 'prb'))
The draws below stay inside these ranges and needn't reach their ends.
Inputs may be any that keep to these rules, and one draw needn't show every extreme that they name: `keep_list`: entries below 4 name distinct beam blocks of the panel; entries equal to 4 are empty slots and stand after the kept ones; each panel keeps between 1 and 3 blocks for each PRB. `alloc`: each PRB lists 64 different users, and every user is listed by some PRB. Owners are device numbers along panel+prb. In each aligned block of 128 rows (PRB-major, then layer), no owner appears more than 8 times.
All inputs are finite; a program needn't handle non-finite values.
Results may differ from the reference program's by a relative error of at most 0.005.
Values may be sent and summed in bfloat16 or wider, within the bound.
A program may use at most 192 MiB of HBM per device.

```python
import math
import jax
import jax.numpy as jnp
import numpy as np
from jax import lax

ANTENNA_EDGE = 8
PANEL_ANTENNAS = 64
NBLK = 4
BB = 16
KMAX = 3
KB = 48
LAYERS_PER_PRB = 64
USERS = 512
RESOURCE_ELEMS = 144
PANEL_TOTAL = 112
PRB_OWN = 2
PRB_DEV = 16
SLOT_PRB_TOTAL = 64
CAP = 8
N_PRB = 4
DEVICES = 32


def draw_keep_list(key, part):
    base = jax.random.fold_in(key, 11)
    first_key, second_key = jax.random.split(base)
    scores = jax.random.randint(first_key, (PANEL_TOTAL, SLOT_PRB_TOTAL, NBLK), 0, 1 << 20) * NBLK + jnp.arange(NBLK, dtype=jnp.int32)
    ordered = jnp.argsort(scores, axis=-1, stable=True)[..., :KMAX].astype(jnp.int32)
    counts = jax.random.randint(second_key, (PANEL_TOTAL, SLOT_PRB_TOTAL, 1), 1, KMAX + 1)
    return jnp.where(jnp.arange(KMAX, dtype=jnp.int32)[None, None, :] < counts, ordered, NBLK).astype(jnp.int32)


def block_scale(key, extent, cuts, low, largest):
    def one(dim, shards_of):
        steps = jax.random.uniform(jax.random.fold_in(jax.random.fold_in(key, 6), dim), (shards_of,), jnp.float32, low / len(cuts), largest / len(cuts))
        return jnp.repeat(jnp.exp(steps), extent[dim] // shards_of).reshape((-1,) + (1,) * (len(extent) - dim - 1))

    gain = one(*cuts[0])
    for cut in cuts[1:]:
        gain = gain * one(*cut)
    return gain


def distinct(key, rows, number_of, top, lift):
    ranking = jax.random.permutation(jax.random.fold_in(key, 1), number_of)
    boost = ranking
    for power in range(3):
        boost = boost * boost // number_of
    boost = boost * lift // number_of
    lots = jax.random.randint(jax.random.fold_in(key, 2), (rows, number_of), 0, 4096) + boost
    sure = jax.random.permutation(jax.random.fold_in(key, 3), rows)[jnp.arange(number_of) % rows]
    lots = jnp.where(jnp.arange(rows)[:, None] == sure[None, :], 1 << 14, lots)
    merit = lots * number_of + jnp.arange(number_of)
    return lax.top_k(merit.astype(jnp.int32), top)[1].astype(jnp.int32)


def deal_out(key, own, number, rows, amount, top, limit, slope):
    sequence = jax.random.permutation(key, amount)
    crowded, ordinary = shares(amount, rows * top, limit, slope, True), shares(amount, rows * top, limit, slope, False)
    places = jnp.arange(amount)

    def named(tallies, rotation):
        used = int((tallies > 0).sum())
        fixed = max(1, used // 4)
        passed = fixed + (places - fixed + rotation * (used - fixed)) % max(1, amount - fixed)
        return jnp.zeros((amount,), jnp.int32).at[sequence[jnp.where(places < fixed, places, passed)]].set(jnp.asarray(tallies, jnp.int32))

    tallies = jnp.where(number % 4 == 0, named(crowded, number // 4), named(ordinary, number - number // 4 - 1))
    mixed = jax.random.permutation(jax.random.fold_in(own, 3), amount)
    source_of, receiver = mixed[0:amount // 2 * 2:2], mixed[1:amount // 2 * 2:2]
    slack = jnp.minimum(tallies[source_of] - 1, limit - tallies[receiver]) // 2
    slack = jnp.where((source_of == sequence[0]) | (receiver == sequence[0]) | (tallies[receiver] == 0), 0, jnp.maximum(slack, 0))
    passed = jax.random.randint(jax.random.fold_in(own, 4), (amount // 2,), 0, 1 << 20) % (slack + 1)
    tallies = tallies.at[source_of].add(-passed).at[receiver].add(passed)
    members = jnp.searchsorted(jnp.cumsum(tallies), jnp.arange(rows * top), side="right").astype(jnp.int32)
    listing = members.reshape(top, rows).T
    listing = listing[jax.random.permutation(jax.random.fold_in(own, 1), rows)]
    rotation = jax.random.randint(jax.random.fold_in(own, 2), (rows, 1), 0, top)
    return jnp.take_along_axis(listing, (jnp.arange(top)[None, :] + rotation) % top, axis=1)


def shares(count, total, bound, lean, full):
    loads = [(1 << 20) // math.isqrt(grade ** lean) + 1 for grade in range(1, count + 1)]
    largest = bound if full else min(bound, max(-(-total // count), total * loads[0] // sum(loads)))
    least = 1 if total - largest >= count - 1 else 0
    holding, rest = [largest] + [least] * (count - 1), total - largest - least * (count - 1)
    while rest > 0:
        movable = [i for i in range(1, count) if holding[i] < largest] or [i for i in range(1, count) if holding[i] < bound]
        whole, left = sum([loads[i] for i in movable]), rest
        for i in movable:
            extra = min(bound - holding[i], max(1, left * loads[i] // whole), rest)
            holding[i] = holding[i] + extra
            rest = rest - extra
    return np.array(holding)


def bell_draw(own_key, shape, scale, limit, cuts=(), held_as=jnp.bfloat16):
    drawn = jax.random.normal(own_key, shape, jnp.float32) * scale
    if len(cuts) > 0:
        drawn = block_scale(own_key, shape, cuts, -0.22, 0.18) * drawn
    return jnp.clip(drawn, min=-limit, max=limit).astype(held_as)


def setup_inputs(seed: int = 0) -> dict:
    seeds = jax.random.split(jax.random.key(seed), 7)
    channel = bell_draw(seeds[0], (PANEL_TOTAL, SLOT_PRB_TOTAL, PANEL_ANTENNAS, 2 * LAYERS_PER_PRB), ((PANEL_TOTAL * 64) ** -0.5), 0.1875, ((0, 8), (1, 4)))
    received = bell_draw(seeds[1], (PANEL_TOTAL, SLOT_PRB_TOTAL, PANEL_ANTENNAS, 2 * RESOURCE_ELEMS), 1.0, 6.0, ((0, 8), (1, 4)))
    keep_list = draw_keep_list(jax.random.fold_in(seeds[6], 71), 0)
    alloc = distinct(seeds[3], SLOT_PRB_TOTAL, USERS, LAYERS_PER_PRB, 0)
    noise_var = jnp.clip(jnp.exp(jax.random.uniform(seeds[4], (USERS,), jnp.float32, math.log(0.1), math.log(1.0))), 0.1, 1.0)
    owner_keys = jax.random.split(jax.random.fold_in(seeds[5], 1), SLOT_PRB_TOTAL * LAYERS_PER_PRB // (PRB_OWN * LAYERS_PER_PRB))
    owner_turns = jax.random.permutation(jax.random.fold_in(seeds[5], 3), SLOT_PRB_TOTAL * LAYERS_PER_PRB // (PRB_OWN * LAYERS_PER_PRB))
    owner = jax.vmap(lambda own, number: deal_out(jax.random.fold_in(seeds[5], 2), own, number, PRB_OWN * LAYERS_PER_PRB, DEVICES, 1, CAP, 2))(owner_keys, owner_turns).reshape((SLOT_PRB_TOTAL, LAYERS_PER_PRB, 1))
    return {"channel": channel, "received": received, "keep_list": keep_list, "alloc": alloc, "noise_var": noise_var, "owner": owner}


def beamspace_tables(panel_side):
    length = panel_side * panel_side
    positions = jnp.arange(length, dtype=jnp.int32)
    first_axis = positions // panel_side
    second_axis = positions % panel_side
    phases = (first_axis[:, None] * first_axis[None, :] + second_axis[:, None] * second_axis[None, :]) % panel_side
    angles = phases.astype(jnp.float32) * (2.0 * math.pi / panel_side)
    real_part = (jnp.cos(angles) / panel_side).astype(jnp.bfloat16)
    imag_part = (-jnp.sin(angles) / panel_side).astype(jnp.bfloat16)
    return (real_part, imag_part)

def combine_parts(first, second, width):
    return jnp.concatenate([first[..., :width] - second[..., width:], second[..., :width] + first[..., width:]], axis=-1).astype(jnp.bfloat16)

def solve_one(factor_one, right_one):
    return jax.scipy.linalg.cho_solve((factor_one, True), right_one)

def solve_layers(products, noise, layer_count, res_count):
    width = layer_count
    block_a = products[:, :width, :width]
    block_b = products[:, :width, width:2 * width]
    block_c = products[:, width:2 * width, :width]
    block_d = products[:, width:2 * width, width:2 * width]
    identity = jnp.eye(width, dtype=jnp.float32)
    gram_real = block_a + block_d + identity[None] * noise[:, :, None]
    gram_imag = block_b - block_c
    system = jnp.concatenate([jnp.concatenate([gram_real, -gram_imag], 2), jnp.concatenate([gram_imag, gram_real], 2)], 1)
    matched = products[:, :, 2 * width:]
    match_real = matched[:, :width, :res_count] + matched[:, width:, res_count:]
    match_imag = matched[:, :width, res_count:] - matched[:, width:, :res_count]
    right_side = jnp.concatenate([match_real, match_imag], 1)
    factor = jnp.linalg.cholesky(system)
    solved = jax.vmap(solve_one)(factor, right_side)
    rows = jnp.concatenate([solved[:, :width], solved[:, width:]], 2)
    return rows.reshape(-1, 2 * res_count)

def reference(channel, received, keep_list, alloc, noise_var, owner):
    beam_table_real, beam_table_imag = beamspace_tables(ANTENNA_EDGE)
    beam_table_real = beam_table_real.astype(jnp.float32)
    beam_table_imag = beam_table_imag.astype(jnp.float32)
    highest = lax.Precision.HIGHEST

    def transform(signal, width):
        first = jnp.einsum('qa,nac->nqc', beam_table_real, signal, precision=highest)
        second = jnp.einsum('qa,nac->nqc', beam_table_imag, signal, precision=highest)
        return combine_parts(first, second, width)

    def per_prb(prb_index):
        channel_prb = lax.dynamic_index_in_dim(channel, prb_index, 1, keepdims=False).astype(jnp.float32)
        signal_prb = lax.dynamic_index_in_dim(received, prb_index, 1, keepdims=False).astype(jnp.float32)
        keep_prb = lax.dynamic_index_in_dim(keep_list, prb_index, 1, keepdims=False)
        beams = jnp.concatenate([transform(channel_prb, LAYERS_PER_PRB), transform(signal_prb, RESOURCE_ELEMS)], axis=-1)
        selector = (keep_prb[:, :, None] == jnp.arange(NBLK, dtype=jnp.int32)[None, None, :]).astype(jnp.float32)
        shaped = beams.astype(jnp.float32).reshape(PANEL_TOTAL, NBLK, BB, beams.shape[-1])
        kept = jnp.einsum('nkb,nbjc->nkjc', selector, shaped, precision=highest).astype(jnp.bfloat16)
        kept_wide = kept.reshape(PANEL_TOTAL, KB, beams.shape[-1]).astype(jnp.float32)
        products = jnp.einsum('nqc,nqd->cd', kept_wide[..., :2 * LAYERS_PER_PRB], kept_wide, precision=highest)
        alloc_row = lax.dynamic_index_in_dim(alloc, prb_index, 0, keepdims=False)
        matches = alloc_row[:, None] == jnp.arange(USERS, dtype=jnp.int32)[None, :]
        noise = jnp.sum(jnp.where(matches, noise_var[None, :], jnp.float32(0.0)), axis=-1)
        return solve_layers(products[None], noise[None], LAYERS_PER_PRB, RESOURCE_ELEMS)
    rows = lax.map(per_prb, jnp.arange(SLOT_PRB_TOTAL, dtype=jnp.int32))
    blocks = SLOT_PRB_TOTAL // PRB_OWN
    block_rows = PRB_OWN * LAYERS_PER_PRB
    rows_blocked = rows.reshape(blocks, block_rows, 2 * RESOURCE_ELEMS)
    owner_blocked = owner.reshape(blocks, block_rows).astype(jnp.int32)
    onehot = (owner_blocked[:, :, None] == jnp.arange(DEVICES, dtype=jnp.int32)[None, None, :]).astype(jnp.int32)
    earlier = jnp.cumsum(onehot, axis=1) - onehot
    slots = jnp.sum(earlier * onehot, axis=2).astype(jnp.int32)
    first_prb = jnp.arange(blocks, dtype=jnp.int32) * PRB_OWN
    source = first_prb % PRB_DEV // PRB_OWN * N_PRB + first_prb // PRB_DEV
    source_rows = jnp.broadcast_to(source[:, None], (blocks, block_rows)).astype(jnp.int32)
    output = jnp.zeros((DEVICES, DEVICES, CAP, 2 * RESOURCE_ELEMS), jnp.float32)
    output = output.at[owner_blocked, source_rows, slots].set(rows_blocked)
    return output.reshape(DEVICES * DEVICES * CAP, 2 * RESOURCE_ELEMS)
```

```python
import functools
import math

import jax
import jax.numpy as jnp
from jax import lax
from jax.experimental import pallas as pl
from jax.experimental.pallas import tpu as pltpu
from jax.sharding import PartitionSpec as P

ANTENNA_EDGE = 8
NBLK = 4


def beam_matrix(panel_side):
    length = panel_side * panel_side
    positions = jnp.arange(length, dtype=jnp.int32)
    first_axis = positions // panel_side
    second_axis = positions % panel_side
    phases = (
        first_axis[:, None] * first_axis[None, :] + second_axis[:, None] * second_axis[None, :]
    ) % panel_side
    angles = phases.astype(jnp.float32) * (2.0 * math.pi / panel_side)
    real_part = (jnp.cos(angles) / panel_side).astype(jnp.bfloat16)
    imag_part = (-jnp.sin(angles) / panel_side).astype(jnp.bfloat16)
    return jnp.concatenate(
        [
            jnp.concatenate([real_part, -imag_part], 1),
            jnp.concatenate([imag_part, real_part], 1),
        ],
        0,
    )


def products_kernel(layers, res, h_ref, y_ref, mask_ref, f_ref, out_ref, left, right):
    panels = h_ref.shape[0]
    stack = f_ref.shape[0]
    lane = lax.broadcasted_iota(jnp.int32, (layers, stack), 1)
    sign = jnp.where(lane < stack // 2, -1.0, 1.0).astype(jnp.bfloat16)
    for n in range(panels):
        h = h_ref[n, 0]
        y = y_ref[n, 0]
        top = jnp.concatenate([y[:, :res], h[:, :layers]], 1)
        low = jnp.concatenate([y[:, res:], h[:, layers:]], 1)
        stacked = jnp.concatenate([top, low], 0)
        beams = jnp.dot(f_ref[...], stacked, preferred_element_type=jnp.float32).astype(
            jnp.bfloat16
        )
        right[n * stack : (n + 1) * stack, :] = beams
        cut = res // 128 * 128
        turned = beams[:, cut:].T[res - cut :]
        turned = turned * mask_ref[0, :, n * stack : (n + 1) * stack]
        swapped = pltpu.roll(turned.astype(jnp.float32), stack // 2, 1).astype(jnp.bfloat16)
        left[:layers, n * stack : (n + 1) * stack] = turned
        left[layers:, n * stack : (n + 1) * stack] = swapped * sign
    out_ref[0] = jnp.dot(left[...], right[...], preferred_element_type=jnp.float32).astype(
        out_ref.dtype
    )


def solve_kernel(
    layers, res, devices, slots, parts_ref, alloc_ref, noise_ref, owner_ref, out_ref, re, im
):
    sources, own = parts_ref.shape[0], parts_ref.shape[1]
    users = noise_ref.shape[1]
    rows = own * layers
    width = layers + res
    cut = res // 128 * 128
    off = res - cut
    first = lax.axis_index("prb") * (own * lax.axis_size("panel")) + lax.axis_index("panel") * own
    highest = lax.Precision.HIGHEST

    row_id = lax.broadcasted_iota(jnp.int32, (layers, 128), 0)
    lane_id = lax.broadcasted_iota(jnp.int32, (layers, 128), 1)
    owners = []
    for p in range(own):
        total = parts_ref[0, p].astype(jnp.float32)
        for s in range(1, sources):
            total = total + parts_ref[s, p].astype(jnp.float32)
        named = alloc_ref[pl.ds(first + p, 1), :]
        picks = (
            lax.broadcasted_iota(jnp.int32, (users, layers), 0) == named
        ).astype(jnp.float32)
        noise = jnp.dot(noise_ref[...], picks, precision=highest)
        spread = jnp.concatenate(
            [jnp.zeros((1, off), jnp.float32), noise, jnp.zeros((1, 128 - off - layers), jnp.float32)],
            1,
        )
        re[p, :, :cut] = total[:layers, :cut]
        im[p, :, :cut] = total[layers:, :cut]
        filler = jnp.zeros((layers, cut + 128 - width), jnp.float32)
        re[p, :, cut:] = jnp.concatenate([total[:layers, cut:], filler], 1) + jnp.where(
            row_id + off == lane_id, spread, 0.0
        )
        im[p, :, cut:] = jnp.concatenate([total[layers:, cut:], filler], 1)
        owners.append(owner_ref[pl.ds(first + p, 1), :])

    def step(k, carry):
        at = jnp.full((layers, 128), 0, jnp.int32) + (k + off)
        for p in range(own):
            a = re[p]
            b = im[p]
            col_r = jnp.take_along_axis(a[:, cut:], at, axis=1)
            col_i = jnp.take_along_axis(b[:, cut:], at, axis=1)
            row_r = re[p, pl.ds(k, 1), :]
            row_i = im[p, pl.ds(k, 1), :]
            tail = jnp.broadcast_to(row_r[:, cut:], (8, 128))
            pivot = jnp.take_along_axis(tail, at[:8], axis=1)
            inverse = 1.0 / pivot[:1]
            inverse = jnp.concatenate([inverse] * (cut // 128 + 1), 1)
            row_r = row_r * inverse
            row_i = row_i * inverse
            col_r = jnp.concatenate([col_r] * (cut // 128 + 1), 1)
            col_i = jnp.concatenate([col_i] * (cut // 128 + 1), 1)
            re[p] = a - (col_r * row_r - col_i * row_i)
            im[p] = b - (col_r * row_i + col_i * row_r)
            re[p, pl.ds(k, 1), :] = row_r
            im[p, pl.ds(k, 1), :] = row_i
        return carry

    lax.fori_loop(0, layers, step, 0)

    owner = jnp.concatenate(owners, 1)
    who = (lax.broadcasted_iota(jnp.int32, (devices, rows), 0) == owner).astype(jnp.float32)
    earlier = (
        lax.broadcasted_iota(jnp.int32, (rows, rows), 0)
        < lax.broadcasted_iota(jnp.int32, (rows, rows), 1)
    ).astype(jnp.bfloat16)
    counts = jnp.dot(who.astype(jnp.bfloat16), earlier, preferred_element_type=jnp.float32)
    slot = jnp.sum(counts * who, axis=0, keepdims=True).astype(jnp.int32)
    target = owner * slots + slot
    place = (
        lax.broadcasted_iota(jnp.int32, (devices * slots, rows), 0) == target
    ).astype(jnp.bfloat16)
    real = jnp.concatenate([re[p, :, :res] for p in range(own)], 0).astype(jnp.bfloat16)
    imag = jnp.concatenate([im[p, :, :res] for p in range(own)], 0).astype(jnp.bfloat16)
    real = jnp.dot(place, real, preferred_element_type=jnp.float32)
    imag = jnp.dot(place, imag, preferred_element_type=jnp.float32)
    out_ref[...] = jnp.concatenate(
        [real.reshape(devices, slots, res), imag.reshape(devices, slots, res)], 1
    ).astype(jnp.bfloat16)


def body(channel, received, keep_list, alloc, noise_var, owner):
    table = beam_matrix(ANTENNA_EDGE)
    layers = channel.shape[-1] // 2
    res = received.shape[-1] // 2
    panels, prb_local, antennas = channel.shape[:3]
    panel_count = lax.axis_size("panel")
    devices = panel_count * lax.axis_size("prb")
    own = prb_local // panel_count
    capacity = max(2, 2 * own * layers // devices)
    slots = -(-capacity // 8) * 8
    stack = 2 * antennas
    width = layers + res

    blocks = jnp.arange(antennas, dtype=jnp.int32) // (antennas // NBLK)
    mask = jnp.any(keep_list[:, :, :, None] == blocks[None, None, None, :], axis=2)
    mask = jnp.concatenate([mask, mask], -1).astype(jnp.bfloat16)
    mask = jnp.transpose(mask, (1, 0, 2)).reshape(prb_local, 1, panels * stack)

    products = pl.pallas_call(
        functools.partial(products_kernel, layers, res),
        out_shape=jax.ShapeDtypeStruct((prb_local, 2 * layers, width), jnp.bfloat16),
        grid=(prb_local,),
        in_specs=[
            pl.BlockSpec((panels, 1, antennas, 2 * layers), lambda p: (0, p, 0, 0)),
            pl.BlockSpec((panels, 1, antennas, 2 * res), lambda p: (0, p, 0, 0)),
            pl.BlockSpec((1, 1, panels * stack), lambda p: (p, 0, 0)),
            pl.BlockSpec((stack, stack), lambda p: (0, 0)),
        ],
        out_specs=pl.BlockSpec((1, 2 * layers, width), lambda p: (p, 0, 0)),
        scratch_shapes=[
            pltpu.VMEM((2 * layers, panels * stack), jnp.bfloat16),
            pltpu.VMEM((panels * stack, width), jnp.bfloat16),
        ],
        compiler_params=pltpu.CompilerParams(vmem_limit_bytes=48 << 20),
    )(channel, received, mask, table)

    parts = lax.all_to_all(
        products.reshape(panel_count, own, 2 * layers, width), "panel", 0, 0, tiled=True
    )
    outgoing = pl.pallas_call(
        functools.partial(solve_kernel, layers, res, devices, slots),
        out_shape=jax.ShapeDtypeStruct((devices, 2 * slots, res), jnp.bfloat16),
        in_specs=[pl.BlockSpec(memory_space=pltpu.VMEM)] * 4,
        out_specs=pl.BlockSpec(memory_space=pltpu.VMEM),
        scratch_shapes=[
            pltpu.VMEM((own, layers, res // 128 * 128 + 128), jnp.float32),
            pltpu.VMEM((own, layers, res // 128 * 128 + 128), jnp.float32),
        ],
        compiler_params=pltpu.CompilerParams(vmem_limit_bytes=48 << 20),
    )(parts, alloc, noise_var.reshape(1, -1), owner.reshape(alloc.shape))
    arrived = lax.all_to_all(outgoing, ("panel", "prb"), split_axis=0, concat_axis=0, tiled=True)
    rows = jnp.concatenate(
        [arrived[:, :capacity], arrived[:, slots : slots + capacity]], -1
    ).astype(jnp.float32)
    return rows.reshape(-1, 2 * res)


def solution(mesh):
    placed = (
        P("panel", "prb", None, None),
        P("panel", "prb", None, None),
        P("panel", "prb", None),
        P(),
        P(),
        P(),
    )
    return jax.shard_map(
        body, mesh=mesh, in_specs=placed, out_specs=P(("panel", "prb"), None), check_vma=False
    )
```

```python
import functools
import math

import jax
import jax.numpy as jnp
import numpy as np
from jax import lax
from jax.experimental import pallas as pl
from jax.experimental.pallas import tpu as pltpu
from jax.sharding import PartitionSpec as P

ANTENNA_EDGE = 8
NBLK = 4


def beam_matrix(panel_side):
    positions = np.arange(panel_side * panel_side)
    first_axis = positions // panel_side
    second_axis = positions % panel_side
    phases = (
        first_axis[:, None] * first_axis[None, :] + second_axis[:, None] * second_axis[None, :]
    ) % panel_side
    angles = phases.astype(np.float32) * np.float32(2.0 * math.pi / panel_side)
    real_part = np.cos(angles) / panel_side
    imag_part = -np.sin(angles) / panel_side
    return np.concatenate(
        [
            np.concatenate([real_part, -imag_part], 1),
            np.concatenate([imag_part, real_part], 1),
        ],
        0,
    ).astype(jnp.bfloat16)


def products_kernel(
    layers,
    res,
    own,
    h_ref,
    y_ref,
    keep_ref,
    f_ref,
    out_ref,
    left,
    right,
    masks,
    sent,
    held,
    send_sem,
    recv_sem,
):
    panels = h_ref.shape[0]
    stack = f_ref.shape[0]
    antennas = stack // 2
    kmax = keep_ref.shape[0]
    peers = lax.axis_size("panel")
    me = lax.axis_index("panel")
    turn = pl.program_id(0)
    offset = turn // own + 1
    peer = lax.rem(me + offset, peers)
    part = lax.rem(turn, own)
    barrier = pltpu.get_barrier_semaphore()

    def copy(there, slot, j):
        return pltpu.make_async_remote_copy(
            src_ref=sent.at[there, j],
            dst_ref=held.at[slot, j],
            send_sem=send_sem.at[there, j],
            recv_sem=recv_sem.at[slot, j],
            device_id={"panel": there},
            device_id_type=pl.DeviceIdType.MESH,
        )

    @pl.when(turn == 0)
    def _():
        for step in range(1, peers):
            pl.semaphore_signal(
                barrier,
                inc=1,
                device_id={"panel": lax.rem(me + step, peers)},
                device_id_type=pl.DeviceIdType.MESH,
            )
        block = (
            lax.rem(lax.broadcasted_iota(jnp.int32, (1, stack), 1), antennas)
            // (antennas // NBLK)
        ).astype(jnp.float32)
        names = [keep_ref[k].astype(jnp.float32).T for k in range(kmax)]
        for n in range(panels):
            hit = names[0][:, n : n + 1] == block
            for k in range(1, kmax):
                hit = hit | (names[k][:, n : n + 1] == block)
            masks[:, n * stack : (n + 1) * stack] = jnp.where(hit, 1.0, 0.0)

    lane = lax.broadcasted_iota(jnp.int32, (layers, stack), 1)
    sign = jnp.where(lane < antennas, -1.0, 1.0)
    mask = masks[pl.ds(peer * own + part, 1), :]
    for n in range(panels):
        h = h_ref[n, 0]
        y = y_ref[n, 0]
        top = jnp.concatenate([y[:, :res], h[:, :layers]], 1)
        low = jnp.concatenate([y[:, res:], h[:, layers:]], 1)
        stacked = jnp.concatenate([top, low], 0)
        beams = jnp.dot(f_ref[...], stacked, preferred_element_type=jnp.float32).astype(
            jnp.bfloat16
        )
        right[n * stack : (n + 1) * stack, :] = beams
        cut = res // 128 * 128
        turned = beams[:, cut:].T[res - cut :].astype(jnp.float32)
        turned = turned * mask[:, n * stack : (n + 1) * stack]
        swapped = pltpu.roll(turned, antennas, 1) * sign
        left[:layers, n * stack : (n + 1) * stack] = turned.astype(jnp.bfloat16)
        left[layers:, n * stack : (n + 1) * stack] = swapped.astype(jnp.bfloat16)
    sent[peer, part] = jnp.dot(
        left[...], right[...], preferred_element_type=jnp.float32
    ).astype(sent.dtype)

    @pl.when(turn == 0)
    def _():
        pl.semaphore_wait(barrier, peers - 1)

    @pl.when(offset < peers)
    def _():
        copy(peer, me, part).start()

    @pl.when(turn == pl.num_programs(0) - 1)
    def _():
        for j in range(own):
            total = sent[me, j].astype(jnp.float32)
            for step in range(1, peers):
                source = lax.rem(me + peers - step, peers)
                copy(source, source, j).wait_recv()
                total = total + held[source, j].astype(jnp.float32)
            out_ref[j] = total
        for j in range(own):
            for step in range(1, peers):
                there = lax.rem(me + step, peers)
                copy(there, me, j).wait_send()


def solve_kernel(
    layers,
    res,
    capacity,
    slots,
    parts_ref,
    alloc_ref,
    noise_ref,
    owner_ref,
    out_ref,
    re,
    im,
    sent,
    held,
    send_sem,
    recv_sem,
):
    own = parts_ref.shape[0]
    users = noise_ref.shape[1]
    rows = own * layers
    width = layers + res
    cut = res // 128 * 128
    off = res - cut
    prbs = lax.axis_size("prb")
    devices = lax.axis_size("panel") * prbs
    me = lax.axis_index("panel") * prbs + lax.axis_index("prb")
    first = lax.axis_index("prb") * (own * lax.axis_size("panel")) + lax.axis_index("panel") * own
    highest = lax.Precision.HIGHEST
    barrier = pltpu.get_barrier_semaphore()

    def at_device(there):
        return {"panel": there // prbs, "prb": lax.rem(there, prbs)}

    def copy(there, slot):
        return pltpu.make_async_remote_copy(
            src_ref=sent.at[there],
            dst_ref=held.at[slot],
            send_sem=send_sem.at[there],
            recv_sem=recv_sem.at[slot],
            device_id=at_device(there),
            device_id_type=pl.DeviceIdType.MESH,
        )

    def greet(step, carry):
        pl.semaphore_signal(
            barrier,
            inc=1,
            device_id=at_device(lax.rem(me + step, devices)),
            device_id_type=pl.DeviceIdType.MESH,
        )
        return carry

    lax.fori_loop(1, devices, greet, 0)

    row_id = lax.broadcasted_iota(jnp.int32, (layers, 128), 0)
    lane_id = lax.broadcasted_iota(jnp.int32, (layers, 128), 1)
    owners = []
    for p in range(own):
        total = parts_ref[p]
        named = alloc_ref[pl.ds(first + p, 1), :]
        picks = (
            lax.broadcasted_iota(jnp.int32, (users, layers), 0) == named
        ).astype(jnp.float32)
        noise = jnp.dot(noise_ref[...], picks, precision=highest)
        spread = jnp.concatenate(
            [
                jnp.zeros((1, off), jnp.float32),
                noise,
                jnp.zeros((1, 128 - off - layers), jnp.float32),
            ],
            1,
        )
        re[p, :, :cut] = total[:layers, :cut]
        im[p, :, :cut] = total[layers:, :cut]
        filler = jnp.zeros((layers, cut + 128 - width), jnp.float32)
        re[p, :, cut:] = jnp.concatenate([total[:layers, cut:], filler], 1) + jnp.where(
            row_id + off == lane_id, spread, 0.0
        )
        im[p, :, cut:] = jnp.concatenate([total[layers:, cut:], filler], 1)
        owners.append(owner_ref[pl.ds(first + p, 1), :])

    def wide(x):
        return jnp.concatenate([x] * (cut // 128 + 1), 1)

    def step(half, carry):
        k = half * 2
        at = jnp.zeros((layers, 128), jnp.int32) + (k + off)
        at_next = at + 1

        def pick(x, index):
            return jnp.take_along_axis(x, index, axis=1)

        def pick_row(x, index):
            return pick(jnp.broadcast_to(x[:, cut:], (8, 128)), index[:8])[:1]

        results = []
        for p in range(own):
            a, b = re[p], im[p]
            ar, ai = re[p, pl.ds(k, 1), :], im[p, pl.ds(k, 1), :]
            br, bi = re[p, pl.ds(k + 1, 1), :], im[p, pl.ds(k + 1, 1), :]
            first_pivot = pick_row(ar, at)
            cross_r, cross_i = pick_row(ar, at_next), pick_row(ai, at_next)
            second_pivot = pick_row(br, at_next)
            scale = 1.0 / (
                first_pivot * second_pivot - (cross_r * cross_r + cross_i * cross_i)
            )
            f, g = wide(second_pivot * scale), wide(first_pivot * scale)
            cr, ci = wide(cross_r * scale), wide(cross_i * scale)
            ur = f * ar - (cr * br - ci * bi)
            ui = f * ai - (cr * bi + ci * br)
            vr = g * br - (cr * ar + ci * ai)
            vi = g * bi - (cr * ai - ci * ar)
            c1r, c1i = wide(pick(a[:, cut:], at)), wide(pick(b[:, cut:], at))
            c2r, c2i = wide(pick(a[:, cut:], at_next)), wide(pick(b[:, cut:], at_next))
            na = a - ((c1r * ur - c1i * ui) + (c2r * vr - c2i * vi))
            nb = b - ((c1r * ui + c1i * ur) + (c2r * vi + c2i * vr))
            results.append((na, nb, ur, ui, vr, vi))
        for p in range(own):
            na, nb, ur, ui, vr, vi = results[p]
            re[p] = na
            im[p] = nb
            re[p, pl.ds(k, 1), :] = ur
            im[p, pl.ds(k, 1), :] = ui
            re[p, pl.ds(k + 1, 1), :] = vr
            im[p, pl.ds(k + 1, 1), :] = vi
        return carry

    lax.fori_loop(0, layers // 2, step, 0)

    owner = jnp.concatenate(owners, 1)
    who = (lax.broadcasted_iota(jnp.int32, (devices, rows), 0) == owner).astype(jnp.float32)
    earlier = (
        lax.broadcasted_iota(jnp.int32, (rows, rows), 0)
        < lax.broadcasted_iota(jnp.int32, (rows, rows), 1)
    ).astype(jnp.bfloat16)
    counts = jnp.dot(who.astype(jnp.bfloat16), earlier, preferred_element_type=jnp.float32)
    slot = jnp.sum(counts * who, axis=0, keepdims=True)
    target = owner.astype(jnp.float32) * slots + slot
    place = (
        lax.broadcasted_iota(jnp.int32, (devices * slots, rows), 0).astype(jnp.float32) == target
    ).astype(jnp.bfloat16)
    real = jnp.concatenate([re[p, :, :res] for p in range(own)], 0).astype(jnp.bfloat16)
    imag = jnp.concatenate([im[p, :, :res] for p in range(own)], 0).astype(jnp.bfloat16)
    real = jnp.dot(place, real, preferred_element_type=jnp.float32)
    imag = jnp.dot(place, imag, preferred_element_type=jnp.float32)
    sent[...] = jnp.concatenate(
        [real.reshape(devices, slots, res), imag.reshape(devices, slots, res)], 1
    ).astype(jnp.bfloat16)

    pl.semaphore_wait(barrier, devices - 1)

    def send(step, carry):
        copy(lax.rem(me + step, devices), me).start()
        return carry

    def arrive(step, carry):
        source = lax.rem(me + devices - step, devices)
        copy(source, source).wait_recv()
        return carry

    def leave(step, carry):
        copy(lax.rem(me + step, devices), me).wait_send()
        return carry

    lax.fori_loop(1, devices, send, 0)
    held[me] = sent[me]
    lax.fori_loop(1, devices, arrive, 0)
    rows_in = held[...].astype(jnp.float32)
    out_ref[:, :res] = rows_in[:, :capacity].reshape(devices * capacity, res)
    out_ref[:, res:] = rows_in[:, slots : slots + capacity].reshape(devices * capacity, res)
    lax.fori_loop(1, devices, leave, 0)


def body(channel, received, keep_list, alloc, noise_var, owner):
    table = jnp.asarray(beam_matrix(ANTENNA_EDGE))
    layers = channel.shape[-1] // 2
    res = received.shape[-1] // 2
    panels, prb_local, antennas = channel.shape[:3]
    peers = lax.axis_size("panel")
    devices = peers * lax.axis_size("prb")
    own = prb_local // peers
    capacity = max(2, 2 * own * layers // devices)
    slots = -(-capacity // 8) * 8
    stack = 2 * antennas
    width = layers + res
    kmax = keep_list.shape[-1]

    def prb_of(turn):
        peer = lax.rem(lax.axis_index("panel") + turn // own + 1, peers)
        return peer * own + lax.rem(turn, own)

    totals = pl.pallas_call(
        functools.partial(products_kernel, layers, res, own),
        out_shape=jax.ShapeDtypeStruct((own, 2 * layers, width), jnp.float32),
        grid=(prb_local,),
        in_specs=[
            pl.BlockSpec((panels, 1, antennas, 2 * layers), lambda t: (0, prb_of(t), 0, 0)),
            pl.BlockSpec((panels, 1, antennas, 2 * res), lambda t: (0, prb_of(t), 0, 0)),
            pl.BlockSpec((kmax, panels, prb_local), lambda t: (0, 0, 0)),
            pl.BlockSpec((stack, stack), lambda t: (0, 0)),
        ],
        out_specs=pl.BlockSpec((own, 2 * layers, width), lambda t: (0, 0, 0)),
        scratch_shapes=[
            pltpu.VMEM((2 * layers, panels * stack), jnp.bfloat16),
            pltpu.VMEM((panels * stack, width), jnp.bfloat16),
            pltpu.VMEM((prb_local, panels * stack), jnp.float32),
            pltpu.VMEM((peers, own, 2 * layers, width), jnp.bfloat16),
            pltpu.VMEM((peers, own, 2 * layers, width), jnp.bfloat16),
            pltpu.SemaphoreType.DMA((peers, own)),
            pltpu.SemaphoreType.DMA((peers, own)),
        ],
        compiler_params=pltpu.CompilerParams(
            vmem_limit_bytes=48 << 20, collective_id=0, has_side_effects=True
        ),
    )(channel, received, jnp.transpose(keep_list, (2, 0, 1)), table)

    return pl.pallas_call(
        functools.partial(solve_kernel, layers, res, capacity, slots),
        out_shape=jax.ShapeDtypeStruct((devices * capacity, 2 * res), jnp.float32),
        in_specs=[pl.BlockSpec(memory_space=pltpu.VMEM)] * 4,
        out_specs=pl.BlockSpec(memory_space=pltpu.VMEM),
        scratch_shapes=[
            pltpu.VMEM((own, layers, res // 128 * 128 + 128), jnp.float32),
            pltpu.VMEM((own, layers, res // 128 * 128 + 128), jnp.float32),
            pltpu.VMEM((devices, 2 * slots, res), jnp.bfloat16),
            pltpu.VMEM((devices, 2 * slots, res), jnp.bfloat16),
            pltpu.SemaphoreType.DMA((devices,)),
            pltpu.SemaphoreType.DMA((devices,)),
        ],
        compiler_params=pltpu.CompilerParams(
            vmem_limit_bytes=48 << 20, collective_id=1, has_side_effects=True
        ),
    )(totals, alloc, noise_var.reshape(1, -1), owner.reshape(alloc.shape))


def solution(mesh):
    placed = (
        P("panel", "prb", None, None),
        P("panel", "prb", None, None),
        P("panel", "prb", None),
        P(),
        P(),
        P(),
    )
    return jax.shard_map(
        body, mesh=mesh, in_specs=placed, out_specs=P(("panel", "prb"), None), check_vma=False
    )
```

```python
import functools
import math

import jax
import jax.numpy as jnp
import numpy as np
from jax import lax
from jax.experimental import pallas as pl
from jax.experimental.pallas import tpu as pltpu
from jax.sharding import PartitionSpec as P

ANTENNA_EDGE = 8
NBLK = 4


def beam_matrix(panel_side):
    positions = np.arange(panel_side * panel_side)
    first_axis = positions // panel_side
    second_axis = positions % panel_side
    phases = (
        first_axis[:, None] * first_axis[None, :] + second_axis[:, None] * second_axis[None, :]
    ) % panel_side
    angles = phases.astype(np.float32) * np.float32(2.0 * math.pi / panel_side)
    real_part = np.cos(angles) / panel_side
    imag_part = -np.sin(angles) / panel_side
    return np.concatenate(
        [
            np.concatenate([real_part, -imag_part], 1),
            np.concatenate([imag_part, real_part], 1),
        ],
        0,
    ).astype(jnp.bfloat16)


def partner(me, step, count):
    if count & (count - 1):
        return lax.rem(me + step, count)
    found, bit = 0, 1
    while bit < count:
        mine = lax.rem(me // bit, 2)
        flip = lax.rem(step // bit, 2) if not isinstance(step, int) else step // bit % 2
        found = found + bit * (mine + flip - 2 * mine * flip)
        bit *= 2
    return found


def partner_back(me, step, count):
    if count & (count - 1):
        return lax.rem(me + count - step, count)
    return partner(me, step, count)


def products_kernel(
    layers,
    res,
    own,
    h_ref,
    y_ref,
    keep_ref,
    f_ref,
    out_ref,
    left,
    right,
    masks,
    sent,
    held,
    send_sem,
    recv_sem,
):
    panels = h_ref.shape[0]
    stack = f_ref.shape[0]
    antennas = stack // 2
    kmax = keep_ref.shape[0]
    peers = lax.axis_size("panel")
    me = lax.axis_index("panel")
    turn = pl.program_id(0)
    offset = peers - 1 - turn // own
    peer = partner(me, offset, peers)
    part = lax.rem(turn, own)
    barrier = pltpu.get_barrier_semaphore()

    def copy(there, slot, j):
        return pltpu.make_async_remote_copy(
            src_ref=sent.at[there, j],
            dst_ref=held.at[slot, j],
            send_sem=send_sem.at[there, j],
            recv_sem=recv_sem.at[slot, j],
            device_id={"panel": there},
            device_id_type=pl.DeviceIdType.MESH,
        )

    @pl.when(turn == 0)
    def _():
        for step in range(1, peers):
            pl.semaphore_signal(
                barrier,
                inc=1,
                device_id={"panel": partner(me, step, peers)},
                device_id_type=pl.DeviceIdType.MESH,
            )
        block = (
            lax.rem(lax.broadcasted_iota(jnp.int32, (1, stack), 1), antennas)
            // (antennas // NBLK)
        ).astype(jnp.float32)
        names = [keep_ref[k].astype(jnp.float32).T for k in range(kmax)]
        for n in range(panels):
            hit = names[0][:, n : n + 1] == block
            for k in range(1, kmax):
                hit = hit | (names[k][:, n : n + 1] == block)
            masks[:, n * stack : (n + 1) * stack] = jnp.where(hit, 1.0, 0.0)

    cut = res // 128 * 128
    lane = lax.broadcasted_iota(jnp.int32, (layers, stack), 1)
    sign = jnp.where(lane < antennas, -1.0, 1.0)
    mask = masks[pl.ds(peer * own + part, 1), :]
    for n in range(panels):
        h = h_ref[n, 0]
        y = y_ref[n, 0]
        top = jnp.concatenate([y[:, :res], h[:, :layers]], 1)
        low = jnp.concatenate([y[:, res:], h[:, layers:]], 1)
        stacked = jnp.concatenate([top, low], 0)
        beams = jnp.dot(f_ref[...], stacked, preferred_element_type=jnp.float32).astype(
            jnp.bfloat16
        )
        right[n * stack : (n + 1) * stack, :] = beams
        turned = beams[:, cut:].T[res - cut :].astype(jnp.float32)
        turned = turned * mask[:, n * stack : (n + 1) * stack]
        swapped = pltpu.roll(turned, antennas, 1) * sign
        left[:layers, n * stack : (n + 1) * stack] = turned.astype(jnp.bfloat16)
        left[layers:, n * stack : (n + 1) * stack] = swapped.astype(jnp.bfloat16)
    result = jnp.dot(left[...], right[...], preferred_element_type=jnp.float32)
    off = res - cut
    filler = jnp.zeros((layers, cut + 128 - layers - res), jnp.float32)
    real = jnp.concatenate([result[:layers, cut:], filler], 1)
    imag = jnp.concatenate([result[layers:, cut:], filler], 1)
    row_id = lax.broadcasted_iota(jnp.int32, (layers, 128), 0)
    lane_id = lax.broadcasted_iota(jnp.int32, (layers, 128), 1)
    mixed = jnp.where(
        lane_id >= off + layers,
        pltpu.roll(imag, off + layers, 1),
        jnp.where(row_id + off < lane_id, imag, real),
    )
    sent[peer, part, :, :cut] = result[:layers, :cut].astype(sent.dtype)
    sent[peer, part, :, cut : 2 * cut] = result[layers:, :cut].astype(sent.dtype)
    sent[peer, part, :, 2 * cut :] = mixed.astype(sent.dtype)

    @pl.when(turn == 0)
    def _():
        pl.semaphore_wait(barrier, peers - 1)

    @pl.when(offset > 0)
    def _():
        copy(peer, me, part).start()

    @pl.when(turn == pl.num_programs(0) - 1)
    def _():
        for j in range(own):
            total = sent[me, j].astype(jnp.float32)
            for step in range(1, peers):
                source = partner_back(me, peers - step, peers)
                copy(source, source, j).wait_recv()
                total = total + held[source, j].astype(jnp.float32)
            out_ref[j] = total
        for j in range(own):
            for step in range(1, peers):
                there = partner(me, peers - step, peers)
                copy(there, me, j).wait_send()


def solve_kernel(
    layers,
    res,
    capacity,
    slots,
    parts_ref,
    alloc_ref,
    noise_ref,
    owner_ref,
    out_ref,
    re,
    im,
    sent,
    held,
    send_sem,
    recv_sem,
):
    own = parts_ref.shape[0]
    users = noise_ref.shape[1]
    rows = own * layers
    cut = res // 128 * 128
    off = res - cut
    prbs = lax.axis_size("prb")
    devices = lax.axis_size("panel") * prbs
    me = lax.axis_index("panel") * prbs + lax.axis_index("prb")
    first = lax.axis_index("prb") * (own * lax.axis_size("panel")) + lax.axis_index("panel") * own
    highest = lax.Precision.HIGHEST
    barrier = pltpu.get_barrier_semaphore()

    def at_device(there):
        return {"panel": there // prbs, "prb": lax.rem(there, prbs)}

    def copy(there, slot):
        return pltpu.make_async_remote_copy(
            src_ref=sent.at[there],
            dst_ref=held.at[slot],
            send_sem=send_sem.at[there],
            recv_sem=recv_sem.at[slot],
            device_id=at_device(there),
            device_id_type=pl.DeviceIdType.MESH,
        )

    def greet(step, carry):
        pl.semaphore_signal(
            barrier,
            inc=1,
            device_id=at_device(lax.rem(me + step, devices)),
            device_id_type=pl.DeviceIdType.MESH,
        )
        return carry

    lax.fori_loop(1, devices, greet, 0)

    row_id = lax.broadcasted_iota(jnp.int32, (layers, 128), 0)
    lane_id = lax.broadcasted_iota(jnp.int32, (layers, 128), 1)
    owners = []
    for p in range(own):
        total = parts_ref[p]
        named = alloc_ref[pl.ds(first + p, 1), :]
        picks = (
            lax.broadcasted_iota(jnp.int32, (users, layers), 0) == named
        ).astype(jnp.float32)
        noise = jnp.dot(noise_ref[...], picks, precision=highest)
        spread = jnp.concatenate(
            [
                jnp.zeros((1, off), jnp.float32),
                noise,
                jnp.zeros((1, 128 - off - layers), jnp.float32),
            ],
            1,
        )
        re[p, :, :cut] = total[:, :cut]
        im[p, :, :cut] = total[:, cut : 2 * cut]
        mixed = total[:, 2 * cut :]
        turned = jnp.concatenate([mixed, jnp.zeros((128 - layers, 128), jnp.float32)], 0).T
        turned = pltpu.roll(turned[off : off + layers], off, 1)
        re[p, :, cut:] = jnp.where(
            row_id + off < lane_id,
            turned,
            jnp.where(row_id + off == lane_id, mixed + spread, mixed),
        )
        im[p, :, cut:] = jnp.where(
            lane_id < off,
            pltpu.roll(mixed, 128 - off - layers, 1),
            jnp.where(
                row_id + off < lane_id,
                mixed,
                jnp.where(row_id + off == lane_id, 0.0, -turned),
            ),
        )
        owners.append(owner_ref[pl.ds(first + p, 1), :])

    def wide(x):
        return jnp.concatenate([x] * (cut // 128 + 1), 1)

    def step(half, carry):
        k = half * 2
        at = jnp.zeros((layers, 128), jnp.int32) + (k + off)
        at_next = at + 1

        def pick(x, index):
            return jnp.take_along_axis(x, index, axis=1)

        def pick_row(x, index):
            return pick(jnp.broadcast_to(x[:, cut:], (8, 128)), index[:8])[:1]

        results = []
        for p in range(own):
            a, b = re[p], im[p]
            ar, ai = re[p, pl.ds(k, 1), :], im[p, pl.ds(k, 1), :]
            br, bi = re[p, pl.ds(k + 1, 1), :], im[p, pl.ds(k + 1, 1), :]
            first_pivot = pick_row(ar, at)
            cross_r, cross_i = pick_row(ar, at_next), pick_row(ai, at_next)
            second_pivot = pick_row(br, at_next)
            scale = 1.0 / (
                first_pivot * second_pivot - (cross_r * cross_r + cross_i * cross_i)
            )
            f, g = wide(second_pivot * scale), wide(first_pivot * scale)
            cr, ci = wide(cross_r * scale), wide(cross_i * scale)
            ur = f * ar - (cr * br - ci * bi)
            ui = f * ai - (cr * bi + ci * br)
            vr = g * br - (cr * ar + ci * ai)
            vi = g * bi - (cr * ai - ci * ar)
            c1r, c1i = wide(pick(a[:, cut:], at)), wide(pick(b[:, cut:], at))
            c2r, c2i = wide(pick(a[:, cut:], at_next)), wide(pick(b[:, cut:], at_next))
            na = a - ((c1r * ur - c1i * ui) + (c2r * vr - c2i * vi))
            nb = b - ((c1r * ui + c1i * ur) + (c2r * vi + c2i * vr))
            results.append((na, nb, ur, ui, vr, vi))
        for p in range(own):
            na, nb, ur, ui, vr, vi = results[p]
            re[p] = na
            im[p] = nb
            re[p, pl.ds(k, 1), :] = ur
            im[p, pl.ds(k, 1), :] = ui
            re[p, pl.ds(k + 1, 1), :] = vr
            im[p, pl.ds(k + 1, 1), :] = vi
        return carry

    lax.fori_loop(0, layers // 2, step, 0)

    owner = jnp.concatenate(owners, 1)
    who = (lax.broadcasted_iota(jnp.int32, (devices, rows), 0) == owner).astype(jnp.float32)
    earlier = (
        lax.broadcasted_iota(jnp.int32, (rows, rows), 0)
        < lax.broadcasted_iota(jnp.int32, (rows, rows), 1)
    ).astype(jnp.bfloat16)
    counts = jnp.dot(who.astype(jnp.bfloat16), earlier, preferred_element_type=jnp.float32)
    slot = jnp.sum(counts * who, axis=0, keepdims=True)
    target = owner.astype(jnp.float32) * slots + slot
    place = (
        lax.broadcasted_iota(jnp.int32, (devices * slots, rows), 0).astype(jnp.float32) == target
    ).astype(jnp.bfloat16)
    real = jnp.concatenate([re[p, :, :res] for p in range(own)], 0).astype(jnp.bfloat16)
    imag = jnp.concatenate([im[p, :, :res] for p in range(own)], 0).astype(jnp.bfloat16)
    real = jnp.dot(place, real, preferred_element_type=jnp.float32)
    imag = jnp.dot(place, imag, preferred_element_type=jnp.float32)
    sent[...] = jnp.concatenate(
        [real.reshape(devices, slots, res), imag.reshape(devices, slots, res)], 1
    ).astype(jnp.bfloat16)

    pl.semaphore_wait(barrier, devices - 1)

    def send(step, carry):
        copy(lax.rem(me + step, devices), me).start()
        return carry

    def arrive(step, carry):
        source = lax.rem(me + devices - step, devices)
        copy(source, source).wait_recv()
        return carry

    def leave(step, carry):
        copy(lax.rem(me + step, devices), me).wait_send()
        return carry

    lax.fori_loop(1, devices, send, 0)
    held[me] = sent[me]
    lax.fori_loop(1, devices, arrive, 0)
    rows_in = held[...].astype(jnp.float32)
    out_ref[:, :res] = rows_in[:, :capacity].reshape(devices * capacity, res)
    out_ref[:, res:] = rows_in[:, slots : slots + capacity].reshape(devices * capacity, res)
    lax.fori_loop(1, devices, leave, 0)


def body(channel, received, keep_list, alloc, noise_var, owner):
    table = jnp.asarray(beam_matrix(ANTENNA_EDGE))
    layers = channel.shape[-1] // 2
    res = received.shape[-1] // 2
    panels, prb_local, antennas = channel.shape[:3]
    peers = lax.axis_size("panel")
    devices = peers * lax.axis_size("prb")
    own = prb_local // peers
    capacity = max(2, 2 * own * layers // devices)
    slots = -(-capacity // 8) * 8
    stack = 2 * antennas
    width = layers + res
    packed = 2 * (res // 128 * 128) + 128
    kmax = keep_list.shape[-1]

    def prb_of(turn):
        peer = partner(lax.axis_index("panel"), peers - 1 - turn // own, peers)
        return peer * own + lax.rem(turn, own)

    totals = pl.pallas_call(
        functools.partial(products_kernel, layers, res, own),
        out_shape=jax.ShapeDtypeStruct((own, layers, packed), jnp.float32),
        grid=(prb_local,),
        in_specs=[
            pl.BlockSpec((panels, 1, antennas, 2 * layers), lambda t: (0, prb_of(t), 0, 0)),
            pl.BlockSpec((panels, 1, antennas, 2 * res), lambda t: (0, prb_of(t), 0, 0)),
            pl.BlockSpec((kmax, panels, prb_local), lambda t: (0, 0, 0)),
            pl.BlockSpec((stack, stack), lambda t: (0, 0)),
        ],
        out_specs=pl.BlockSpec((own, layers, packed), lambda t: (0, 0, 0)),
        scratch_shapes=[
            pltpu.VMEM((2 * layers, panels * stack), jnp.bfloat16),
            pltpu.VMEM((panels * stack, width), jnp.bfloat16),
            pltpu.VMEM((prb_local, panels * stack), jnp.float32),
            pltpu.VMEM((peers, own, layers, packed), jnp.bfloat16),
            pltpu.VMEM((peers, own, layers, packed), jnp.bfloat16),
            pltpu.SemaphoreType.DMA((peers, own)),
            pltpu.SemaphoreType.DMA((peers, own)),
        ],
        compiler_params=pltpu.CompilerParams(
            vmem_limit_bytes=63 << 20, collective_id=0, has_side_effects=True
        ),
    )(channel, received, jnp.transpose(keep_list, (2, 0, 1)), table)

    return pl.pallas_call(
        functools.partial(solve_kernel, layers, res, capacity, slots),
        out_shape=jax.ShapeDtypeStruct((devices * capacity, 2 * res), jnp.float32),
        in_specs=[pl.BlockSpec(memory_space=pltpu.VMEM)] * 4,
        out_specs=pl.BlockSpec(memory_space=pltpu.VMEM),
        scratch_shapes=[
            pltpu.VMEM((own, layers, res // 128 * 128 + 128), jnp.float32),
            pltpu.VMEM((own, layers, res // 128 * 128 + 128), jnp.float32),
            pltpu.VMEM((devices, 2 * slots, res), jnp.bfloat16),
            pltpu.VMEM((devices, 2 * slots, res), jnp.bfloat16),
            pltpu.SemaphoreType.DMA((devices,)),
            pltpu.SemaphoreType.DMA((devices,)),
        ],
        compiler_params=pltpu.CompilerParams(
            vmem_limit_bytes=48 << 20, collective_id=1, has_side_effects=True
        ),
    )(totals, alloc, noise_var.reshape(1, -1), owner.reshape(alloc.shape))


def solution(mesh):
    placed = (
        P("panel", "prb", None, None),
        P("panel", "prb", None, None),
        P("panel", "prb", None),
        P(),
        P(),
        P(),
    )
    return jax.shard_map(
        body, mesh=mesh, in_specs=placed, out_specs=P(("panel", "prb"), None), check_vma=False
    )
```

```python
import functools
import math

import jax
import jax.numpy as jnp
import numpy as np
from jax import lax
from jax.experimental import pallas as pl
from jax.experimental.pallas import tpu as pltpu
from jax.sharding import PartitionSpec as P

ANTENNA_EDGE = 8
NBLK = 4
GROUP = 4


def beam_matrix(panel_side):
    positions = np.arange(panel_side * panel_side)
    first_axis = positions // panel_side
    second_axis = positions % panel_side
    phases = (
        first_axis[:, None] * first_axis[None, :] + second_axis[:, None] * second_axis[None, :]
    ) % panel_side
    angles = phases.astype(np.float32) * np.float32(2.0 * math.pi / panel_side)
    real_part = np.cos(angles) / panel_side
    imag_part = -np.sin(angles) / panel_side
    return np.concatenate(
        [
            np.concatenate([real_part, -imag_part], 1),
            np.concatenate([imag_part, real_part], 1),
        ],
        0,
    ).astype(jnp.bfloat16)


def partner(me, step, count):
    if count & (count - 1):
        return lax.rem(me + step, count)
    found, bit = 0, 1
    while bit < count:
        mine = lax.rem(me // bit, 2)
        flip = lax.rem(step // bit, 2) if not isinstance(step, int) else step // bit % 2
        found = found + bit * (mine + flip - 2 * mine * flip)
        bit *= 2
    return found


def partner_back(me, step, count):
    if count & (count - 1):
        return lax.rem(me + count - step, count)
    return partner(me, step, count)


def products_kernel(
    layers,
    res,
    own,
    h_ref,
    y_ref,
    keep_ref,
    f_ref,
    out_ref,
    left,
    right,
    masks,
    sent,
    held,
    send_sem,
    recv_sem,
):
    panels = h_ref.shape[0]
    stack = f_ref.shape[0]
    antennas = stack // 2
    kmax = keep_ref.shape[0]
    peers = lax.axis_size("panel")
    me = lax.axis_index("panel")
    turn = pl.program_id(0)
    offset = peers - 1 - turn // own
    peer = partner(me, offset, peers)
    part = lax.rem(turn, own)
    barrier = pltpu.get_barrier_semaphore()

    def copy(there, slot, j):
        return pltpu.make_async_remote_copy(
            src_ref=sent.at[there, j],
            dst_ref=held.at[slot, j],
            send_sem=send_sem.at[there, j],
            recv_sem=recv_sem.at[slot, j],
            device_id={"panel": there},
            device_id_type=pl.DeviceIdType.MESH,
        )

    @pl.when(turn == 0)
    def _():
        for step in range(1, peers):
            pl.semaphore_signal(
                barrier,
                inc=1,
                device_id={"panel": partner(me, step, peers)},
                device_id_type=pl.DeviceIdType.MESH,
            )
        block = (
            lax.rem(lax.broadcasted_iota(jnp.int32, (1, stack), 1), antennas)
            // (antennas // NBLK)
        ).astype(jnp.float32)
        names = [keep_ref[k].astype(jnp.float32).T for k in range(kmax)]
        for n in range(panels):
            hit = names[0][:, n : n + 1] == block
            for k in range(1, kmax):
                hit = hit | (names[k][:, n : n + 1] == block)
            masks[:, n * stack : (n + 1) * stack] = jnp.where(hit, 1.0, 0.0)

    cut = res // 128 * 128
    lane = lax.broadcasted_iota(jnp.int32, (layers, stack), 1)
    sign = jnp.where(lane < antennas, -1.0, 1.0)
    mask = masks[pl.ds(peer * own + part, 1), :]
    result = None
    done = 0
    for n in range(panels):
        h = h_ref[n, 0]
        y = y_ref[n, 0]
        top = jnp.concatenate([y[:, :res], h[:, :layers]], 1)
        low = jnp.concatenate([y[:, res:], h[:, layers:]], 1)
        stacked = jnp.concatenate([top, low], 0)
        beams = jnp.dot(f_ref[...], stacked, preferred_element_type=jnp.float32).astype(
            jnp.bfloat16
        )
        right[n * stack : (n + 1) * stack, :] = beams
        turned = beams[:, cut:].T[res - cut :].astype(jnp.float32)
        turned = turned * mask[:, n * stack : (n + 1) * stack]
        swapped = pltpu.roll(turned, antennas, 1) * sign
        left[:layers, n * stack : (n + 1) * stack] = turned.astype(jnp.bfloat16)
        left[layers:, n * stack : (n + 1) * stack] = swapped.astype(jnp.bfloat16)
        if n % GROUP == GROUP - 1 or n == panels - 1:
            here = slice(done * stack, (n + 1) * stack)
            term = jnp.dot(left[:, here], right[here, :], preferred_element_type=jnp.float32)
            result = term if result is None else result + term
            done = n + 1
    off = res - cut
    filler = jnp.zeros((layers, cut + 128 - layers - res), jnp.float32)
    real = jnp.concatenate([result[:layers, cut:], filler], 1)
    imag = jnp.concatenate([result[layers:, cut:], filler], 1)
    row_id = lax.broadcasted_iota(jnp.int32, (layers, 128), 0)
    lane_id = lax.broadcasted_iota(jnp.int32, (layers, 128), 1)
    mixed = jnp.where(
        lane_id >= off + layers,
        pltpu.roll(imag, off + layers, 1),
        jnp.where(row_id + off < lane_id, imag, real),
    )
    sent[peer, part, :, :cut] = result[:layers, :cut].astype(sent.dtype)
    sent[peer, part, :, cut : 2 * cut] = result[layers:, :cut].astype(sent.dtype)
    sent[peer, part, :, 2 * cut :] = mixed.astype(sent.dtype)

    @pl.when(turn == 0)
    def _():
        pl.semaphore_wait(barrier, peers - 1)

    @pl.when(offset > 0)
    def _():
        copy(peer, me, part).start()

    @pl.when(turn == pl.num_programs(0) - 1)
    def _():
        for j in range(own):
            total = sent[me, j].astype(jnp.float32)
            for step in range(1, peers):
                source = partner_back(me, peers - step, peers)
                copy(source, source, j).wait_recv()
                total = total + held[source, j].astype(jnp.float32)
            out_ref[j] = total
        for j in range(own):
            for step in range(1, peers):
                there = partner(me, peers - step, peers)
                copy(there, me, j).wait_send()


def solve_kernel(
    layers,
    res,
    capacity,
    slots,
    parts_ref,
    alloc_ref,
    noise_ref,
    owner_ref,
    out_ref,
    re,
    im,
    sent,
    held,
    send_sem,
    recv_sem,
):
    own = parts_ref.shape[0]
    users = noise_ref.shape[1]
    rows = own * layers
    cut = res // 128 * 128
    off = res - cut
    prbs = lax.axis_size("prb")
    devices = lax.axis_size("panel") * prbs
    me = lax.axis_index("panel") * prbs + lax.axis_index("prb")
    first = lax.axis_index("prb") * (own * lax.axis_size("panel")) + lax.axis_index("panel") * own
    highest = lax.Precision.HIGHEST
    barrier = pltpu.get_barrier_semaphore()

    def at_device(there):
        return {"panel": there // prbs, "prb": lax.rem(there, prbs)}

    def copy(there, slot):
        return pltpu.make_async_remote_copy(
            src_ref=sent.at[there],
            dst_ref=held.at[slot],
            send_sem=send_sem.at[there],
            recv_sem=recv_sem.at[slot],
            device_id=at_device(there),
            device_id_type=pl.DeviceIdType.MESH,
        )

    def greet(step, carry):
        pl.semaphore_signal(
            barrier,
            inc=1,
            device_id=at_device(lax.rem(me + step, devices)),
            device_id_type=pl.DeviceIdType.MESH,
        )
        return carry

    lax.fori_loop(1, devices, greet, 0)

    row_id = lax.broadcasted_iota(jnp.int32, (layers, 128), 0)
    lane_id = lax.broadcasted_iota(jnp.int32, (layers, 128), 1)
    owners = []
    for p in range(own):
        total = parts_ref[p]
        named = alloc_ref[pl.ds(first + p, 1), :]
        picks = (
            lax.broadcasted_iota(jnp.int32, (users, layers), 0) == named
        ).astype(jnp.float32)
        noise = jnp.dot(noise_ref[...], picks, precision=highest)
        spread = jnp.concatenate(
            [
                jnp.zeros((1, off), jnp.float32),
                noise,
                jnp.zeros((1, 128 - off - layers), jnp.float32),
            ],
            1,
        )
        re[p, :, :cut] = total[:, :cut]
        im[p, :, :cut] = total[:, cut : 2 * cut]
        mixed = total[:, 2 * cut :]
        turned = jnp.concatenate([mixed, jnp.zeros((128 - layers, 128), jnp.float32)], 0).T
        turned = pltpu.roll(turned[off : off + layers], off, 1)
        re[p, :, cut:] = jnp.where(
            row_id + off < lane_id,
            turned,
            jnp.where(row_id + off == lane_id, mixed + spread, mixed),
        )
        im[p, :, cut:] = jnp.where(
            lane_id < off,
            pltpu.roll(mixed, 128 - off - layers, 1),
            jnp.where(
                row_id + off < lane_id,
                mixed,
                jnp.where(row_id + off == lane_id, 0.0, -turned),
            ),
        )
        owners.append(owner_ref[pl.ds(first + p, 1), :])

    def wide(x):
        return jnp.concatenate([x] * (cut // 128 + 1), 1)

    def step(half, carry):
        k = half * 2
        at = jnp.zeros((layers, 128), jnp.int32) + (k + off)
        at_next = at + 1

        def pick(x, index):
            return jnp.take_along_axis(x, index, axis=1)

        def pick_row(x, index):
            return pick(jnp.broadcast_to(x[:, cut:], (8, 128)), index[:8])[:1]

        results = []
        for p in range(own):
            a, b = re[p], im[p]
            ar, ai = re[p, pl.ds(k, 1), :], im[p, pl.ds(k, 1), :]
            br, bi = re[p, pl.ds(k + 1, 1), :], im[p, pl.ds(k + 1, 1), :]
            first_pivot = pick_row(ar, at)
            cross_r, cross_i = pick_row(ar, at_next), pick_row(ai, at_next)
            second_pivot = pick_row(br, at_next)
            scale = 1.0 / (
                first_pivot * second_pivot - (cross_r * cross_r + cross_i * cross_i)
            )
            f, g = wide(second_pivot * scale), wide(first_pivot * scale)
            cr, ci = wide(cross_r * scale), wide(cross_i * scale)
            ur = f * ar - (cr * br - ci * bi)
            ui = f * ai - (cr * bi + ci * br)
            vr = g * br - (cr * ar + ci * ai)
            vi = g * bi - (cr * ai - ci * ar)
            c1r, c1i = wide(pick(a[:, cut:], at)), wide(pick(b[:, cut:], at))
            c2r, c2i = wide(pick(a[:, cut:], at_next)), wide(pick(b[:, cut:], at_next))
            na = a - ((c1r * ur - c1i * ui) + (c2r * vr - c2i * vi))
            nb = b - ((c1r * ui + c1i * ur) + (c2r * vi + c2i * vr))
            results.append((na, nb, ur, ui, vr, vi))
        for p in range(own):
            na, nb, ur, ui, vr, vi = results[p]
            re[p] = na
            im[p] = nb
            re[p, pl.ds(k, 1), :] = ur
            im[p, pl.ds(k, 1), :] = ui
            re[p, pl.ds(k + 1, 1), :] = vr
            im[p, pl.ds(k + 1, 1), :] = vi
        return carry

    lax.fori_loop(0, layers // 2, step, 0)

    owner = jnp.concatenate(owners, 1)
    who = (lax.broadcasted_iota(jnp.int32, (devices, rows), 0) == owner).astype(jnp.float32)
    earlier = (
        lax.broadcasted_iota(jnp.int32, (rows, rows), 0)
        < lax.broadcasted_iota(jnp.int32, (rows, rows), 1)
    ).astype(jnp.bfloat16)
    counts = jnp.dot(who.astype(jnp.bfloat16), earlier, preferred_element_type=jnp.float32)
    slot = jnp.sum(counts * who, axis=0, keepdims=True)
    target = owner.astype(jnp.float32) * slots + slot
    place = (
        lax.broadcasted_iota(jnp.int32, (devices * slots, rows), 0).astype(jnp.float32) == target
    ).astype(jnp.bfloat16)
    real = jnp.concatenate([re[p, :, :res] for p in range(own)], 0).astype(jnp.bfloat16)
    imag = jnp.concatenate([im[p, :, :res] for p in range(own)], 0).astype(jnp.bfloat16)
    real = jnp.dot(place, real, preferred_element_type=jnp.float32)
    imag = jnp.dot(place, imag, preferred_element_type=jnp.float32)
    sent[...] = jnp.concatenate(
        [real.reshape(devices, slots, res), imag.reshape(devices, slots, res)], 1
    ).astype(jnp.bfloat16)

    pl.semaphore_wait(barrier, devices - 1)

    def send(step, carry):
        copy(lax.rem(me + step, devices), me).start()
        return carry

    def arrive(step, carry):
        source = lax.rem(me + devices - step, devices)
        copy(source, source).wait_recv()
        return carry

    def leave(step, carry):
        copy(lax.rem(me + step, devices), me).wait_send()
        return carry

    lax.fori_loop(1, devices, send, 0)
    held[me] = sent[me]
    lax.fori_loop(1, devices, arrive, 0)
    rows_in = held[...].astype(jnp.float32)
    out_ref[:, :res] = rows_in[:, :capacity].reshape(devices * capacity, res)
    out_ref[:, res:] = rows_in[:, slots : slots + capacity].reshape(devices * capacity, res)
    lax.fori_loop(1, devices, leave, 0)


def body(channel, received, keep_list, alloc, noise_var, owner):
    table = jnp.asarray(beam_matrix(ANTENNA_EDGE))
    layers = channel.shape[-1] // 2
    res = received.shape[-1] // 2
    panels, prb_local, antennas = channel.shape[:3]
    peers = lax.axis_size("panel")
    devices = peers * lax.axis_size("prb")
    own = prb_local // peers
    capacity = max(2, 2 * own * layers // devices)
    slots = -(-capacity // 8) * 8
    stack = 2 * antennas
    width = layers + res
    packed = 2 * (res // 128 * 128) + 128
    kmax = keep_list.shape[-1]

    def prb_of(turn):
        peer = partner(lax.axis_index("panel"), peers - 1 - turn // own, peers)
        return peer * own + lax.rem(turn, own)

    totals = pl.pallas_call(
        functools.partial(products_kernel, layers, res, own),
        out_shape=jax.ShapeDtypeStruct((own, layers, packed), jnp.float32),
        grid=(prb_local,),
        in_specs=[
            pl.BlockSpec((panels, 1, antennas, 2 * layers), lambda t: (0, prb_of(t), 0, 0)),
            pl.BlockSpec((panels, 1, antennas, 2 * res), lambda t: (0, prb_of(t), 0, 0)),
            pl.BlockSpec((kmax, panels, prb_local), lambda t: (0, 0, 0)),
            pl.BlockSpec((stack, stack), lambda t: (0, 0)),
        ],
        out_specs=pl.BlockSpec((own, layers, packed), lambda t: (0, 0, 0)),
        scratch_shapes=[
            pltpu.VMEM((2 * layers, panels * stack), jnp.bfloat16),
            pltpu.VMEM((panels * stack, width), jnp.bfloat16),
            pltpu.VMEM((prb_local, panels * stack), jnp.float32),
            pltpu.VMEM((peers, own, layers, packed), jnp.bfloat16),
            pltpu.VMEM((peers, own, layers, packed), jnp.bfloat16),
            pltpu.SemaphoreType.DMA((peers, own)),
            pltpu.SemaphoreType.DMA((peers, own)),
        ],
        compiler_params=pltpu.CompilerParams(
            vmem_limit_bytes=63 << 20, collective_id=0, has_side_effects=True
        ),
    )(channel, received, jnp.transpose(keep_list, (2, 0, 1)), table)

    return pl.pallas_call(
        functools.partial(solve_kernel, layers, res, capacity, slots),
        out_shape=jax.ShapeDtypeStruct((devices * capacity, 2 * res), jnp.float32),
        in_specs=[pl.BlockSpec(memory_space=pltpu.VMEM)] * 4,
        out_specs=pl.BlockSpec(memory_space=pltpu.VMEM),
        scratch_shapes=[
            pltpu.VMEM((own, layers, res // 128 * 128 + 128), jnp.float32),
            pltpu.VMEM((own, layers, res // 128 * 128 + 128), jnp.float32),
            pltpu.VMEM((devices, 2 * slots, res), jnp.bfloat16),
            pltpu.VMEM((devices, 2 * slots, res), jnp.bfloat16),
            pltpu.SemaphoreType.DMA((devices,)),
            pltpu.SemaphoreType.DMA((devices,)),
        ],
        compiler_params=pltpu.CompilerParams(
            vmem_limit_bytes=48 << 20, collective_id=1, has_side_effects=True
        ),
    )(totals, alloc, noise_var.reshape(1, -1), owner.reshape(alloc.shape))


def solution(mesh):
    placed = (
        P("panel", "prb", None, None),
        P("panel", "prb", None, None),
        P("panel", "prb", None),
        P(),
        P(),
        P(),
    )
    return jax.shard_map(
        body, mesh=mesh, in_specs=placed, out_specs=P(("panel", "prb"), None), check_vma=False
    )
```
